32 devices in a mesh: groups: 2 (over x), band: 16 (over z, y, core).
Axes of the slice: x: 2, y: 2, z: 4, core: 2. Of those that a mesh axis runs over, the one named last changes fastest.
Arguments:
- tile_blocks: bfloat16 [256, 32, 128, 128], P(('groups', 'band')), parts along dimension 0, may hold values from -0.09375 to 0.09375
- column_ids: int32 [256, 32], P(('groups', 'band')), parts along dimension 0, may hold values from 0 to 383, as said below
- arc_cost: float32 [98304], P(('groups', 'band')), parts along dimension 0, may hold values from 0.25 to 4
- demand_rhs: float32 [32768, 128], P(('groups', 'band')), parts along dimension 0, may hold values from -6 to 6
- primal_start: float32 [98304, 128], P(('groups', 'band')), parts along dimension 0, may hold values from 0.05 to 2
- dual_start: float32 [32768, 128], P(('groups', 'band')), parts along dimension 0, may hold values from -6 to 6
Outputs:
- primal_next: float32 [98304, 128], P(('groups', 'band')), parts along dimension 0
- dual_next: float32 [32768, 128], P(('groups', 'band')), parts along dimension 0
- relative_gap: float32 [256], P('groups'), parts along dimension 0
The draws below stay inside these ranges and needn't reach their ends.
There are 2 independent parts, one for each index of `groups`. The reference program is written for one: setup_inputs(seed, part) draws one part's arguments, and reference() takes and returns one part's arrays. A program takes and returns all parts, laid end to end along the dimension named above; each array names one. Nothing has to cross between parts.
Inputs may be any that keep to these rules, and one draw needn't show every extreme that they name: `column_ids`: row block g lies in band r = g // 8; bands have 24 column blocks each and are counted cyclically. Its 32 column blocks are distinct: the first 6 among the last 8 blocks of band r - 1, the next 20 in band r, the last 6 among the first 8 blocks of band r + 1.
All inputs are finite; a program needn't handle non-finite values.
Results may differ from the reference program's by a relative error of at most 0.0011.
Values may be sent and summed in bfloat16 or wider, within the bound.
A program may use at most 128 MiB of HBM per device.

```python
import math
import jax
import jax.numpy as jnp
from jax import lax

BLK = 128
RBD = 8
CBD = 24
MB = 8
LEFT_TILES = 6
OWN_TILES = 20
RIGHT_TILES = 6
SCEN = 128
TILES = 32
NRB = 128
NROWS = 16384
NCOLS = 49152
N_BAND = 16


def draw_column_ids(key, part):
    count = RBD * N_BAND
    rows = jnp.arange(count, dtype=jnp.int32)
    band_of = rows // RBD
    key_left = jax.random.fold_in(key, 11)
    key_own = jax.random.fold_in(key, 12)
    key_right = jax.random.fold_in(key, 13)
    left_pick = jax.vmap(lambda k: jax.random.permutation(k, MB)[:LEFT_TILES])(jax.random.split(key_left, count))
    own_pick = jax.vmap(lambda k: jax.random.permutation(k, CBD)[:OWN_TILES])(jax.random.split(key_own, count))
    right_pick = jax.vmap(lambda k: jax.random.permutation(k, MB)[:RIGHT_TILES])(jax.random.split(key_right, count))
    left_ids = ((band_of - 1) % N_BAND)[:, None] * CBD + (CBD - MB) + left_pick.astype(jnp.int32)
    own_ids = band_of[:, None] * CBD + own_pick.astype(jnp.int32)
    right_ids = ((band_of + 1) % N_BAND)[:, None] * CBD + right_pick.astype(jnp.int32)
    return jnp.concatenate([left_ids, own_ids, right_ids], axis=1).astype(jnp.int32)


def block_scale(key, dims, cuts, least, top_value):
    loudness, own = 1.0, jax.random.fold_in(key, 6)
    for dim, parts in cuts:
        draws = jnp.exp(jax.random.uniform(jax.random.fold_in(own, dim), (parts,), jnp.float32, least / len(cuts), top_value / len(cuts)))
        loudness = loudness * jnp.repeat(draws, dims[dim] // parts).reshape([-1 if axis == dim else 1 for axis in range(len(dims))])
    return loudness


def bell_draw(rng, shape, spread, most, shards=(), held_as=jnp.bfloat16):
    factor_of = block_scale(rng, shape, shards, -0.22, 0.18) if shards else 1.0
    values = jax.random.normal(rng, shape, jnp.float32) * spread * factor_of
    return jnp.minimum(jnp.maximum(values, -most), most).astype(held_as)


def setup_inputs(seed: int = 0, part: int = 0) -> dict:
    key_of = jax.random.split(jax.random.key(seed), 7)
    own_keys = jax.random.split(jax.random.fold_in(key_of[6], part), 7)
    tile_blocks = bell_draw(own_keys[0], (NRB, TILES, BLK, BLK), (TILES * BLK) ** -0.5, 0.09375, ((0, 16),))
    column_ids = draw_column_ids(jax.random.fold_in(jax.random.fold_in(key_of[6], part), 71), part)
    arc_cost = jnp.clip(jnp.exp(math.log(4.0) - 2.7725887 * jax.random.uniform(own_keys[2], (NCOLS,), jnp.float32) ** block_scale(own_keys[2], (NCOLS,), ((0, 16),), -0.2, 0.2)), 0.25, 4.0)
    demand_rhs = bell_draw(own_keys[3], (NROWS, SCEN), 1.0, 6.0, ((0, 16),), jnp.float32)
    primal_start = jnp.clip(jnp.exp(math.log(2.0) - 3.6888794 * jax.random.uniform(own_keys[4], (NCOLS, SCEN), jnp.float32) ** block_scale(own_keys[4], (NCOLS, SCEN), ((0, 16),), -0.2, 0.2)), 0.05, 2.0)
    dual_start = bell_draw(own_keys[5], (NROWS, SCEN), 1.0, 6.0, ((0, 16),), jnp.float32)
    return dict(tile_blocks=tile_blocks, column_ids=column_ids, arc_cost=arc_cost, demand_rhs=demand_rhs, primal_start=primal_start, dual_start=dual_start)


def forward_product(tile_blocks, column_ids, flow_blocks):

    def row_product(items):
        tile_row, id_row = items
        picked = flow_blocks[id_row].astype(jnp.float32)
        return jnp.einsum('tij,tjs->is', tile_row.astype(jnp.float32), picked)
    result = lax.map(row_product, (tile_blocks, column_ids))
    return result.reshape(-1, SCEN)

def adjoint_product(tile_blocks, column_ids, dual_blocks):
    start = jnp.zeros((N_BAND, CBD, BLK, SCEN), jnp.float32)
    tiles_band = tile_blocks.reshape(N_BAND, RBD, TILES, BLK, BLK)
    ids_band = column_ids.reshape(N_BAND, RBD, TILES)
    duals_band = dual_blocks.reshape(N_BAND, RBD, BLK, SCEN)
    bands = jnp.arange(N_BAND, dtype=jnp.int32)

    def band_step(total, items):
        band, tiles, ids, duals = items
        local = ((ids - (band * CBD - MB)) % (CBD * N_BAND)).astype(jnp.int32)

        def add_row(window, row_items):
            tile_row, id_row, dual_row = row_items
            terms = jnp.einsum('tji,js->tis', tile_row.astype(jnp.float32), dual_row.astype(jnp.float32))
            return (window.at[id_row].add(terms), None)
        window, unused = lax.scan(add_row, jnp.zeros((CBD + 2 * MB, BLK, SCEN), jnp.float32), (tiles, local, duals))
        own_part = window[MB:MB + CBD]
        left_part = lax.optimization_barrier(window[:MB].astype(jnp.bfloat16)).astype(jnp.float32)
        right_part = lax.optimization_barrier(window[MB + CBD:].astype(jnp.bfloat16)).astype(jnp.float32)
        total = total.at[band].add(own_part)
        total = total.at[(band - 1) % N_BAND, CBD - MB:].add(left_part)
        total = total.at[(band + 1) % N_BAND, :MB].add(right_part)
        return (total, None)
    total, unused = lax.scan(band_step, start, (bands, tiles_band, ids_band, duals_band))
    return total.reshape(-1, SCEN)

def reference(tile_blocks, column_ids, arc_cost, demand_rhs, primal_start, dual_start):
    cost_sq = jnp.sum(arc_cost * arc_cost)
    rhs_sq = lax.optimization_barrier(jnp.sum(demand_rhs * demand_rhs, axis=0))
    omega = jnp.sqrt(cost_sq / (rhs_sq + 1e-06))
    tau = 0.3 / omega
    sigma = 0.3 * omega
    flow_round = primal_start.astype(jnp.bfloat16).reshape(-1, BLK, SCEN)
    dual_mid = dual_start + sigma * (demand_rhs - forward_product(tile_blocks, column_ids, flow_round))
    dual_round = dual_mid.astype(jnp.bfloat16).reshape(-1, BLK, SCEN)
    adjoint = adjoint_product(tile_blocks, column_ids, dual_round)
    primal_next = jnp.maximum(primal_start - tau * (arc_cost[:, None] - adjoint), 0.0)
    extrapolated = (2.0 * primal_next - primal_start).astype(jnp.bfloat16).reshape(-1, BLK, SCEN)
    dual_next = dual_mid + sigma * (demand_rhs - forward_product(tile_blocks, column_ids, extrapolated))
    primal_obj = lax.optimization_barrier(jnp.sum(arc_cost[:, None] * primal_next, axis=0))
    dual_obj = lax.optimization_barrier(jnp.sum(demand_rhs * dual_next, axis=0))
    relative_gap = (primal_obj - dual_obj) / (1.0 + jnp.abs(primal_obj) + jnp.abs(dual_obj))
    return (primal_next, dual_next, relative_gap)
```

```python
import functools

import jax
import jax.numpy as jnp
from jax import lax
from jax.experimental import pallas as pl
from jax.experimental.pallas import tpu as pltpu
from jax.sharding import PartitionSpec as P

MB = 8
BLK = 128
PAIR = 2 * BLK
F32 = jnp.float32
BF16 = jnp.bfloat16
MESH = pl.DeviceIdType.MESH


def kernel(
    n,
    tiles_hbm,
    ids_ref,
    cost_ref,
    rhs_hbm,
    primal_hbm,
    dual_hbm,
    primal_out,
    dual_out,
    gap_out,
    *scratch,
):
    row_blocks, tile_count = ids_ref.shape
    tiles = scratch[:row_blocks]
    (
        dense,
        inv_v,
        inv_s,
        primal,
        cost_col,
        rhs,
        dual,
        acc,
        flow,
        flow2,
        halo_l,
        halo_r,
        halo2_l,
        halo2_r,
        send_l,
        send_r,
        term_l,
        term_r,
        own_adj,
        norm_buf,
        obj_buf,
        tile_sem,
        in_sem,
        inv_sem,
        out_sem,
        halo_send,
        halo_recv,
        norm_send,
        norm_recv,
        obj_send,
        obj_recv,
    ) = scratch[row_blocks:]
    rows = row_blocks * BLK
    ends = MB // 2
    own = primal_hbm.shape[0] // PAIR
    pairs = own + 2 * ends
    col_blocks = 2 * own
    total_blocks = col_blocks * n
    end_rows = ends * PAIR
    mid_rows = (own - 2 * ends) * PAIR

    me = lax.axis_index("band")
    left = lax.rem(me + n - 1, n)
    right = lax.rem(me + 1, n)

    barrier = pltpu.get_barrier_semaphore()

    def greet(k, carry):
        pl.semaphore_signal(
            barrier, inc=1, device_id={"band": lax.rem(me + k, n)}, device_id_type=MESH
        )
        return carry

    lax.fori_loop(1, n, greet, None)

    def load_rows(start, size, k):
        return pltpu.make_async_copy(
            primal_hbm.at[pl.ds(start, size)], primal.at[pl.ds(start, size)], in_sem.at[k]
        )

    head = load_rows(0, end_rows, 0)
    tail = load_rows(end_rows + mid_rows, end_rows, 1)
    middle = load_rows(end_rows, mid_rows, 2)
    rhs_in = pltpu.make_async_copy(rhs_hbm, rhs, in_sem.at[3])
    dual_in = pltpu.make_async_copy(dual_hbm, dual, in_sem.at[4])
    tile_in = [
        pltpu.make_async_copy(
            tiles_hbm.at[g], tiles[g].at[pl.ds(0, tile_count)], tile_sem.at[g]
        )
        for g in range(row_blocks)
    ]
    head.start()
    tail.start()
    rhs_in.start()
    for copy in tile_in[:2]:
        copy.start()
    middle.start()
    for copy in tile_in[2:]:
        copy.start()
    dual_in.start()

    base = me * col_blocks - MB
    local = lax.rem(ids_ref[...] - base + total_blocks, total_blocks)
    lane = lax.broadcasted_iota(jnp.int32, (row_blocks, BLK), 1)
    inverse = jnp.full((row_blocks, BLK), tile_count, jnp.int32)
    for t in range(tile_count):
        inverse = jnp.where(lane == local[:, t : t + 1], t, inverse)
    inv_v[...] = inverse
    inv_copy = pltpu.make_async_copy(inv_v, inv_s, inv_sem)
    inv_copy.start()

    def exchange(kind, side, c, source, target):
        index = (kind * 2 + side) * ends + c
        return pltpu.make_async_remote_copy(
            src_ref=source,
            dst_ref=target,
            send_sem=halo_send.at[index],
            recv_sem=halo_recv.at[index],
            device_id={"band": left if side == 0 else right},
            device_id_type=MESH,
        )

    to_left = [exchange(0, 0, c, flow.at[c], halo_r.at[c]) for c in range(ends)]
    to_right = [
        exchange(0, 1, c, flow.at[own - ends + c], halo_l.at[c]) for c in range(ends)
    ]
    head.wait()
    for c in range(ends):
        flow[c] = primal[c * PAIR : (c + 1) * PAIR].astype(BF16)
    tail.wait()
    for c in range(own - ends, own):
        flow[c] = primal[c * PAIR : (c + 1) * PAIR].astype(BF16)
    pl.semaphore_wait(barrier, n - 1)
    for c in range(ends):
        to_left[c].start()
        to_right[c].start()

    def share(buf, send_sems, recv_sems, k):
        peer = lax.rem(me + k, n)
        return pltpu.make_async_remote_copy(
            src_ref=buf.at[me],
            dst_ref=buf.at[me],
            send_sem=send_sems.at[peer],
            recv_sem=recv_sems.at[me],
            device_id={"band": peer},
            device_id_type=MESH,
        )

    def collect(buf, send_sems, recv_sems, k):
        peer = lax.rem(me + k, n)
        return pltpu.make_async_remote_copy(
            src_ref=buf.at[peer],
            dst_ref=buf.at[peer],
            send_sem=send_sems.at[peer],
            recv_sem=recv_sems.at[peer],
            device_id={"band": peer},
            device_id_type=MESH,
        )

    def share_all(buf, send_sems, recv_sems):
        def step(k, carry):
            share(buf, send_sems, recv_sems, k).start()
            return carry

        lax.fori_loop(1, n, step, None)

    def collect_all(buf, send_sems, recv_sems):
        def step(k, carry):
            copy = collect(buf, send_sems, recv_sems, k)
            copy.wait_recv()
            copy.wait_send()
            return carry

        lax.fori_loop(1, n, step, None)
        return jnp.sum(buf[...], axis=0)

    def stack(first, second):
        return jnp.concatenate([first, second, jnp.zeros((6, BLK), F32)], axis=0)

    rhs_in.wait()
    rhs_sq = jnp.sum(rhs[...] * rhs[...], axis=0, keepdims=True)
    cost_sq = jnp.sum(cost_ref[...] * cost_ref[...], axis=0, keepdims=True)
    norm_buf[me] = stack(rhs_sq, cost_sq)
    share_all(norm_buf, norm_send, norm_recv)

    for w in range(col_blocks):
        cost_col[w * BLK : (w + 1) * BLK] = jnp.transpose(
            jnp.broadcast_to(cost_ref[w : w + 1, :], (BLK, BLK))
        )
    middle.wait()
    for c in range(ends, own - ends):
        flow[c] = primal[c * PAIR : (c + 1) * PAIR].astype(BF16)

    inv_copy.wait()
    for g in range(row_blocks):
        tiles[g][tile_count] = jnp.zeros((BLK, BLK), BF16)
        tile_in[g].wait()

        def place(p, carry, g=g):
            for half in range(2):
                dense[p, g * BLK : (g + 1) * BLK, half * BLK : (half + 1) * BLK] = tiles[g][
                    inv_s[g, 2 * p + half]
                ]
            return carry

        lax.fori_loop(0, pairs, place, None, unroll=4)

    def product(p, block):
        return jnp.dot(dense[p], block, preferred_element_type=F32)

    acc[...] = product(ends, flow[0])

    def own_step(p, carry):
        acc[...] += product(ends + p, flow[p])
        return carry

    lax.fori_loop(1, own, own_step, None)
    for c in range(ends):
        to_right[c].wait_recv()
        acc[...] += product(c, halo_l[c])
        to_left[c].wait_recv()
        acc[...] += product(ends + own + c, halo_r[c])

    norms = collect_all(norm_buf, norm_send, norm_recv)
    cost_total = jnp.sum(norms[1:2], axis=1, keepdims=True)
    omega = jnp.sqrt(cost_total / (norms[0:1] + 1e-06))
    tau = 0.3 / omega
    sigma = 0.3 * omega

    dual_in.wait()
    dual_mid = dual[...] + sigma * (rhs[...] - acc[...])
    dual[...] = dual_mid
    dual_t = jnp.transpose(dual_mid).astype(BF16)

    def adjoint(p):
        flat = jnp.dot(dual_t, dense[p], preferred_element_type=F32)
        return jnp.transpose(flat)

    terms_left = [exchange(1, 0, c, send_l.at[c], term_r.at[c]) for c in range(ends)]
    terms_right = [exchange(1, 1, c, send_r.at[c], term_l.at[c]) for c in range(ends)]
    for c in range(ends):
        send_l[c] = adjoint(c).astype(BF16)
        terms_left[c].start()
        send_r[c] = adjoint(ends + own + c).astype(BF16)
        terms_right[c].start()

    for c in range(ends):
        own_adj[c] = adjoint(ends + c)
        own_adj[ends + c] = adjoint(own + c)

    def advance(p, total):
        span = slice(p * PAIR, (p + 1) * PAIR)
        start = primal[span]
        cost = cost_col[span]
        following = jnp.maximum(start - tau * (cost - total), 0.0)
        flow2[p] = (2.0 * following - start).astype(BF16)
        primal[span] = following
        store = pltpu.make_async_copy(
            primal.at[pl.ds(p * PAIR, PAIR)],
            primal_out.at[pl.ds(p * PAIR, PAIR)],
            out_sem.at[p],
        )
        store.start()
        return store, jnp.sum(cost * following, axis=0, keepdims=True)

    stores = []
    primal_obj = jnp.zeros((1, BLK), F32)
    for p in range(ends, own - ends):
        store, part = advance(p, adjoint(ends + p))
        stores.append(store)
        primal_obj += part
    acc[...] = product(2 * ends, flow2[ends])
    for p in range(ends + 1, own - ends):
        acc[...] += product(ends + p, flow2[p])

    flow_left = [exchange(2, 0, c, flow2.at[c], halo2_r.at[c]) for c in range(ends)]
    flow_right = [
        exchange(2, 1, c, flow2.at[own - ends + c], halo2_l.at[c]) for c in range(ends)
    ]
    for c in range(ends):
        terms_right[c].wait_recv()
        store, part = advance(c, own_adj[c] + term_l[c].astype(F32))
        stores.append(store)
        primal_obj += part
        flow_left[c].start()
        terms_left[c].wait_recv()
        store, part = advance(own - ends + c, own_adj[ends + c] + term_r[c].astype(F32))
        stores.append(store)
        primal_obj += part
        flow_right[c].start()
    for c in range(ends):
        acc[...] += product(ends + c, flow2[c])
        acc[...] += product(own + c, flow2[own - ends + c])
    for c in range(ends):
        flow_right[c].wait_recv()
        acc[...] += product(c, halo2_l[c])
        flow_left[c].wait_recv()
        acc[...] += product(ends + own + c, halo2_r[c])

    dual_next = dual[...] + sigma * (rhs[...] - acc[...])
    acc[...] = dual_next
    dual_store = pltpu.make_async_copy(acc, dual_out, in_sem.at[5])
    dual_store.start()
    dual_obj = jnp.sum(rhs[...] * dual_next, axis=0, keepdims=True)
    obj_buf[me] = stack(primal_obj, dual_obj)
    share_all(obj_buf, obj_send, obj_recv)
    for copy in to_left + to_right + terms_left + terms_right + flow_left + flow_right:
        copy.wait_send()
    for store in stores:
        store.wait()
    totals = collect_all(obj_buf, obj_send, obj_recv)
    primal_total = totals[0:1]
    dual_total = totals[1:2]
    gap_out[...] = (primal_total - dual_total) / (
        1.0 + jnp.abs(primal_total) + jnp.abs(dual_total)
    )
    dual_store.wait()


def per_device(n, tile_blocks, column_ids, arc_cost, demand_rhs, primal_start, dual_start):
    row_blocks, tile_count = column_ids.shape
    cols, scen = primal_start.shape
    rows = demand_rhs.shape[0]
    own = cols // PAIR
    ends = MB // 2
    pairs = own + 2 * ends
    any_space = pl.BlockSpec(memory_space=pl.ANY)
    vmem = pl.BlockSpec(memory_space=pltpu.VMEM)
    halo = pltpu.VMEM((ends, PAIR, scen), BF16)
    dma = pltpu.SemaphoreType.DMA
    scratch = [pltpu.VMEM((tile_count + 1, BLK, BLK), BF16) for _ in range(row_blocks)]
    scratch += [
        pltpu.VMEM((pairs, rows, PAIR), BF16),
        pltpu.VMEM((row_blocks, BLK), jnp.int32),
        pltpu.SMEM((row_blocks, BLK), jnp.int32),
        pltpu.VMEM((cols, scen), F32),
        pltpu.VMEM((cols, scen), F32),
        pltpu.VMEM((rows, scen), F32),
        pltpu.VMEM((rows, scen), F32),
        pltpu.VMEM((rows, scen), F32),
        pltpu.VMEM((own, PAIR, scen), BF16),
        pltpu.VMEM((own, PAIR, scen), BF16),
        halo,
        halo,
        halo,
        halo,
        halo,
        halo,
        halo,
        halo,
        pltpu.VMEM((2 * ends, PAIR, scen), F32),
        pltpu.VMEM((n, 8, scen), F32),
        pltpu.VMEM((n, 8, scen), F32),
        dma((row_blocks,)),
        dma((6,)),
        dma,
        dma((own,)),
        dma((6 * ends,)),
        dma((6 * ends,)),
        dma((n,)),
        dma((n,)),
        dma((n,)),
        dma((n,)),
    ]
    flops = 3 * 2 * pairs * PAIR * rows * scen
    primal_next, dual_next, gap = pl.pallas_call(
        functools.partial(kernel, n),
        out_shape=(
            jax.ShapeDtypeStruct((cols, scen), F32),
            jax.ShapeDtypeStruct((rows, scen), F32),
            jax.ShapeDtypeStruct((1, scen), F32),
        ),
        in_specs=[any_space, vmem, vmem, any_space, any_space, any_space],
        out_specs=(any_space, any_space, vmem),
        scratch_shapes=scratch,
        compiler_params=pltpu.CompilerParams(
            collective_id=0, has_side_effects=True, vmem_limit_bytes=48 * 1024 * 1024
        ),
        cost_estimate=pl.CostEstimate(
            flops=flops, bytes_accessed=2 * tile_blocks.size + 8 * cols * scen, transcendentals=0
        ),
    )(
        tile_blocks,
        column_ids,
        arc_cost.reshape(cols // BLK, BLK),
        demand_rhs,
        primal_start,
        dual_start,
    )
    return primal_next, dual_next, gap.reshape(scen)


def solution(mesh):
    in_specs = (
        P(("groups", "band"), None, None, None),
        P(("groups", "band"), None),
        P(("groups", "band")),
        P(("groups", "band"), None),
        P(("groups", "band"), None),
        P(("groups", "band"), None),
    )
    out_specs = (P(("groups", "band"), None), P(("groups", "band"), None), P("groups"))
    return jax.shard_map(
        functools.partial(per_device, mesh.shape["band"]),
        mesh=mesh,
        in_specs=in_specs,
        out_specs=out_specs,
        check_vma=False,
    )
```

```python
import functools

import jax
import jax.numpy as jnp
from jax import lax
from jax.experimental import pallas as pl
from jax.experimental.pallas import tpu as pltpu
from jax.sharding import PartitionSpec as P

MB = 8
BLK = 128
PAIR = 2 * BLK
F32 = jnp.float32
BF16 = jnp.bfloat16
MESH = pl.DeviceIdType.MESH


def kernel(
    n,
    tiles_hbm,
    ids_ref,
    cost_ref,
    rhs_hbm,
    primal_hbm,
    dual_hbm,
    primal_out,
    dual_out,
    totals_out,
    *scratch,
):
    row_blocks, tile_count = ids_ref.shape
    tiles = scratch[:row_blocks]
    (
        dense,
        inv_v,
        inv_s,
        primal,
        cost_col,
        rhs,
        dual,
        acc,
        flow,
        flow2,
        halo_l,
        halo_r,
        halo2_l,
        halo2_r,
        send_l,
        send_r,
        term_l,
        term_r,
        own_adj,
        norm_buf,
        obj_buf,
        tile_sem,
        in_sem,
        inv_sem,
        halo_send,
        halo_recv,
        norm_send,
        norm_recv,
        obj_send,
        obj_recv,
    ) = scratch[row_blocks:]
    rows = row_blocks * BLK
    ends = MB // 2
    own = primal_hbm.shape[0] // PAIR
    pairs = own + 2 * ends
    col_blocks = 2 * own
    total_blocks = col_blocks * n
    end_rows = ends * PAIR
    mid_rows = (own - 2 * ends) * PAIR

    me = lax.axis_index("band")
    left = lax.rem(me + n - 1, n)
    right = lax.rem(me + 1, n)

    barrier = pltpu.get_barrier_semaphore()

    def greet(k, carry):
        pl.semaphore_signal(
            barrier, inc=1, device_id={"band": lax.rem(me + k, n)}, device_id_type=MESH
        )
        return carry

    lax.fori_loop(1, n, greet, None)

    def load_rows(start, size, k):
        return pltpu.make_async_copy(
            primal_hbm.at[pl.ds(start, size)], primal.at[pl.ds(start, size)], in_sem.at[k]
        )

    head = load_rows(0, end_rows, 0)
    tail = load_rows(end_rows + mid_rows, end_rows, 1)
    middle = load_rows(end_rows, mid_rows, 2)
    rhs_in = pltpu.make_async_copy(rhs_hbm, rhs, in_sem.at[3])
    dual_in = pltpu.make_async_copy(dual_hbm, dual, in_sem.at[4])
    tile_in = [
        pltpu.make_async_copy(
            tiles_hbm.at[g], tiles[g].at[pl.ds(0, tile_count)], tile_sem.at[g]
        )
        for g in range(row_blocks)
    ]
    head.start()
    tail.start()
    rhs_in.start()
    for copy in tile_in[:2]:
        copy.start()
    middle.start()
    for copy in tile_in[2:]:
        copy.start()
    dual_in.start()

    base = me * col_blocks - MB
    local = lax.rem(ids_ref[...] - base + total_blocks, total_blocks)
    lane = lax.broadcasted_iota(jnp.int32, (row_blocks, BLK), 1)
    inverse = jnp.full((row_blocks, BLK), tile_count, jnp.int32)
    for t in range(tile_count):
        inverse = jnp.where(lane == local[:, t : t + 1], t, inverse)
    inv_v[...] = inverse
    inv_copy = pltpu.make_async_copy(inv_v, inv_s, inv_sem)
    inv_copy.start()

    def chunk(ref, c):
        return ref.at[pl.ds(c * PAIR, PAIR)]

    def exchange(kind, side, c, source, target):
        index = (kind * 2 + side) * ends + c
        return pltpu.make_async_remote_copy(
            src_ref=source,
            dst_ref=target,
            send_sem=halo_send.at[index],
            recv_sem=halo_recv.at[index],
            device_id={"band": left if side == 0 else right},
            device_id_type=MESH,
        )

    to_left = [exchange(0, 0, c, chunk(flow, c), chunk(halo_r, c)) for c in range(ends)]
    to_right = [
        exchange(0, 1, c, chunk(flow, own - ends + c), chunk(halo_l, c)) for c in range(ends)
    ]
    head.wait()
    for c in range(ends):
        flow[c * PAIR : (c + 1) * PAIR] = primal[c * PAIR : (c + 1) * PAIR].astype(BF16)
    tail.wait()
    for c in range(own - ends, own):
        flow[c * PAIR : (c + 1) * PAIR] = primal[c * PAIR : (c + 1) * PAIR].astype(BF16)
    pl.semaphore_wait(barrier, n - 1)
    for c in range(ends):
        to_left[c].start()
        to_right[c].start()

    def share(buf, send_sems, recv_sems, k):
        peer = lax.rem(me + k, n)
        return pltpu.make_async_remote_copy(
            src_ref=buf.at[me],
            dst_ref=buf.at[me],
            send_sem=send_sems.at[peer],
            recv_sem=recv_sems.at[me],
            device_id={"band": peer},
            device_id_type=MESH,
        )

    def collect(buf, send_sems, recv_sems, k):
        peer = lax.rem(me + k, n)
        return pltpu.make_async_remote_copy(
            src_ref=buf.at[peer],
            dst_ref=buf.at[peer],
            send_sem=send_sems.at[peer],
            recv_sem=recv_sems.at[peer],
            device_id={"band": peer},
            device_id_type=MESH,
        )

    def share_all(buf, send_sems, recv_sems):
        def step(k, carry):
            share(buf, send_sems, recv_sems, k).start()
            return carry

        lax.fori_loop(1, n, step, None)

    def collect_all(buf, send_sems, recv_sems):
        def step(k, carry):
            copy = collect(buf, send_sems, recv_sems, k)
            copy.wait_recv()
            copy.wait_send()
            return carry

        lax.fori_loop(1, n, step, None)
        return jnp.sum(buf[...], axis=0)

    def stack(first, second):
        return jnp.concatenate([first, second, jnp.zeros((6, BLK), F32)], axis=0)

    rhs_in.wait()
    rhs_sq = jnp.sum(rhs[...] * rhs[...], axis=0, keepdims=True)
    cost_sq = jnp.sum(cost_ref[...] * cost_ref[...], axis=0, keepdims=True)
    norm_buf[me] = stack(rhs_sq, cost_sq)
    share_all(norm_buf, norm_send, norm_recv)

    for w in range(col_blocks):
        cost_col[w * BLK : (w + 1) * BLK] = jnp.transpose(
            jnp.broadcast_to(cost_ref[w : w + 1, :], (BLK, BLK))
        )
    middle.wait()
    for c in range(ends, own - ends):
        flow[c * PAIR : (c + 1) * PAIR] = primal[c * PAIR : (c + 1) * PAIR].astype(BF16)

    inv_copy.wait()
    for g in range(row_blocks):
        tiles[g][tile_count] = jnp.zeros((BLK, BLK), BF16)
        tile_in[g].wait()

        def place(p, carry, g=g):
            for half in range(2):
                start = pl.multiple_of((2 * p + half) * BLK, BLK)
                dense[g * BLK : (g + 1) * BLK, pl.ds(start, BLK)] = tiles[g][
                    inv_s[g, 2 * p + half]
                ]
            return carry

        lax.fori_loop(0, pairs, place, None, unroll=4)

    left_end = end_rows
    right_end = (ends + own) * PAIR
    part_rows = 2 * BLK

    def product(start, block, first=False):
        size = block.shape[0]

        def step(i, carry):
            at = pl.ds(pl.multiple_of(i * part_rows, part_rows), part_rows)
            value = jnp.dot(
                dense[at, start : start + size], block[...], preferred_element_type=F32
            )
            acc[at] = value if first else acc[at] + value
            return carry

        lax.fori_loop(0, rows // part_rows, step, None)

    def halo_products(low, low_copies, high, high_copies):
        half = ends // 2
        for h in range(2):
            for c in range(h * half, (h + 1) * half):
                low_copies[c].wait_recv()
                high_copies[c].wait_recv()
            at = h * half * PAIR
            for i in range(0, rows, part_rows):
                acc[i : i + part_rows] += jnp.dot(
                    dense[i : i + part_rows, at : at + half * PAIR],
                    low[at : at + half * PAIR],
                    preferred_element_type=F32,
                ) + jnp.dot(
                    dense[i : i + part_rows, right_end + at : right_end + at + half * PAIR],
                    high[at : at + half * PAIR],
                    preferred_element_type=F32,
                )

    product(left_end, flow, True)
    halo_products(halo_l, to_right, halo_r, to_left)

    norms = collect_all(norm_buf, norm_send, norm_recv)
    cost_total = jnp.sum(norms[1:2], axis=1, keepdims=True)
    omega = jnp.sqrt(cost_total / (norms[0:1] + 1e-06))
    tau = 0.3 / omega
    sigma = 0.3 * omega

    dual_in.wait()
    dual_mid = dual[...] + sigma * (rhs[...] - acc[...])
    dual[...] = dual_mid
    dual_t = jnp.transpose(dual_mid).astype(BF16)

    def adjoint(p):
        flat = jnp.dot(
            dual_t, dense[:, p * PAIR : (p + 1) * PAIR], preferred_element_type=F32
        )
        return jnp.transpose(flat)

    terms_left = [exchange(1, 0, c, chunk(send_l, c), chunk(term_r, c)) for c in range(ends)]
    terms_right = [exchange(1, 1, c, chunk(send_r, c), chunk(term_l, c)) for c in range(ends)]
    for c in range(ends):
        send_l[c * PAIR : (c + 1) * PAIR] = adjoint(c).astype(BF16)
        terms_left[c].start()
        send_r[c * PAIR : (c + 1) * PAIR] = adjoint(ends + own + c).astype(BF16)
        terms_right[c].start()

    for c in range(ends):
        own_adj[c] = adjoint(ends + c)
        own_adj[ends + c] = adjoint(own + c)

    def advance(p, total):
        span = slice(p * PAIR, (p + 1) * PAIR)
        start = primal[span]
        cost = cost_col[span]
        following = jnp.maximum(start - tau * (cost - total), 0.0)
        flow2[span] = (2.0 * following - start).astype(BF16)
        primal_out[span] = following
        return jnp.sum(cost * following, axis=0, keepdims=True)

    primal_obj = jnp.zeros((1, BLK), F32)
    for p in range(ends, own - ends):
        primal_obj += advance(p, adjoint(ends + p))
    product(left_end + end_rows, flow2.at[pl.ds(end_rows, mid_rows)], True)

    flow_left = [exchange(2, 0, c, chunk(flow2, c), chunk(halo2_r, c)) for c in range(ends)]
    flow_right = [
        exchange(2, 1, c, chunk(flow2, own - ends + c), chunk(halo2_l, c)) for c in range(ends)
    ]
    for c in range(ends):
        terms_right[c].wait_recv()
        primal_obj += advance(c, own_adj[c] + term_l[c * PAIR : (c + 1) * PAIR].astype(F32))
        flow_left[c].start()
        terms_left[c].wait_recv()
        primal_obj += advance(own - ends + c, own_adj[ends + c] + term_r[c * PAIR : (c + 1) * PAIR].astype(F32))
        flow_right[c].start()
    product(left_end, flow2.at[pl.ds(0, end_rows)])
    product(right_end - end_rows, flow2.at[pl.ds(end_rows + mid_rows, end_rows)])
    halo_products(halo2_l, flow_right, halo2_r, flow_left)

    dual_next = dual[...] + sigma * (rhs[...] - acc[...])
    dual_out[...] = dual_next
    dual_obj = jnp.sum(rhs[...] * dual_next, axis=0, keepdims=True)
    obj_buf[me] = stack(primal_obj, dual_obj)
    share_all(obj_buf, obj_send, obj_recv)
    for copy in to_left + to_right + terms_left + terms_right + flow_left + flow_right:
        copy.wait_send()
    totals_out[...] = collect_all(obj_buf, obj_send, obj_recv)


def finish(primal_in, dual_in, totals, primal_out, dual_out, gap_out, sems):
    first = pltpu.make_async_copy(primal_in, primal_out, sems.at[0])
    second = pltpu.make_async_copy(dual_in, dual_out, sems.at[1])
    first.start()
    second.start()
    primal_total = totals[0:1]
    dual_total = totals[1:2]
    gap_out[...] = (primal_total - dual_total) / (
        1.0 + jnp.abs(primal_total) + jnp.abs(dual_total)
    )
    first.wait()
    second.wait()


def per_device(n, tile_blocks, column_ids, arc_cost, demand_rhs, primal_start, dual_start):
    row_blocks, tile_count = column_ids.shape
    cols, scen = primal_start.shape
    rows = demand_rhs.shape[0]
    own = cols // PAIR
    ends = MB // 2
    pairs = own + 2 * ends
    any_space = pl.BlockSpec(memory_space=pl.ANY)
    hbm = pl.BlockSpec(memory_space=pltpu.HBM)
    vmem = pl.BlockSpec(memory_space=pltpu.VMEM)
    halo = pltpu.VMEM((ends * PAIR, scen), BF16)
    dma = pltpu.SemaphoreType.DMA
    scratch = [pltpu.VMEM((tile_count + 1, BLK, BLK), BF16) for _ in range(row_blocks)]
    scratch += [
        pltpu.VMEM((rows, pairs * PAIR), BF16),
        pltpu.VMEM((row_blocks, BLK), jnp.int32),
        pltpu.SMEM((row_blocks, BLK), jnp.int32),
        pltpu.VMEM((cols, scen), F32),
        pltpu.VMEM((cols, scen), F32),
        pltpu.VMEM((rows, scen), F32),
        pltpu.VMEM((rows, scen), F32),
        pltpu.VMEM((rows, scen), F32),
        pltpu.VMEM((cols, scen), BF16),
        pltpu.VMEM((cols, scen), BF16),
        halo,
        halo,
        halo,
        halo,
        halo,
        halo,
        halo,
        halo,
        pltpu.VMEM((2 * ends, PAIR, scen), F32),
        pltpu.VMEM((n, 8, scen), F32),
        pltpu.VMEM((n, 8, scen), F32),
        dma((row_blocks,)),
        dma((5,)),
        dma,
        dma((6 * ends,)),
        dma((6 * ends,)),
        dma((n,)),
        dma((n,)),
        dma((n,)),
        dma((n,)),
    ]
    flops = 3 * 2 * pairs * PAIR * rows * scen
    outs = pl.pallas_call(
        functools.partial(kernel, n),
        out_shape=(
            pltpu.VMEM((cols, scen), F32),
            pltpu.VMEM((rows, scen), F32),
            pltpu.VMEM((8, scen), F32),
        ),
        in_specs=[hbm, vmem, vmem, hbm, hbm, hbm],
        out_specs=(vmem, vmem, vmem),
        scratch_shapes=scratch,
        compiler_params=pltpu.CompilerParams(
            collective_id=0, has_side_effects=True, vmem_limit_bytes=56 * 1024 * 1024
        ),
        cost_estimate=pl.CostEstimate(
            flops=flops, bytes_accessed=2 * tile_blocks.size + 8 * cols * scen, transcendentals=0
        ),
    )(
        tile_blocks,
        column_ids,
        arc_cost.reshape(cols // BLK, BLK),
        demand_rhs,
        primal_start,
        dual_start,
    )
    primal_next, dual_next, gap = pl.pallas_call(
        finish,
        out_shape=(
            jax.ShapeDtypeStruct((cols, scen), F32),
            jax.ShapeDtypeStruct((rows, scen), F32),
            jax.ShapeDtypeStruct((1, scen), F32),
        ),
        in_specs=[any_space, any_space, vmem],
        out_specs=(hbm, hbm, vmem),
        scratch_shapes=[dma((2,))],
        compiler_params=pltpu.CompilerParams(vmem_limit_bytes=1024 * 1024),
    )(*outs)
    return primal_next, dual_next, gap.reshape(scen)


def solution(mesh):
    in_specs = (
        P(("groups", "band"), None, None, None),
        P(("groups", "band"), None),
        P(("groups", "band")),
        P(("groups", "band"), None),
        P(("groups", "band"), None),
        P(("groups", "band"), None),
    )
    out_specs = (P(("groups", "band"), None), P(("groups", "band"), None), P("groups"))
    return jax.shard_map(
        functools.partial(per_device, mesh.shape["band"]),
        mesh=mesh,
        in_specs=in_specs,
        out_specs=out_specs,
        check_vma=False,
    )
```

```python
import functools

import jax
import jax.numpy as jnp
from jax import lax
from jax.experimental import pallas as pl
from jax.experimental.pallas import tpu as pltpu
from jax.sharding import PartitionSpec as P

MB = 8
BLK = 128
PAIR = 2 * BLK
F32 = jnp.float32
BF16 = jnp.bfloat16
MESH = pl.DeviceIdType.MESH


def kernel(
    n,
    tiles_hbm,
    ids_ref,
    cost_ref,
    rhs_hbm,
    primal_hbm,
    dual_hbm,
    primal_out,
    dual_out,
    totals_out,
    *scratch,
):
    row_blocks, tile_count = ids_ref.shape
    tiles = scratch[:row_blocks]
    (
        dense,
        inv_v,
        inv_s,
        primal,
        cost_col,
        rhs,
        dual,
        acc,
        flow,
        flow2,
        halo_l,
        halo_r,
        halo2_l,
        halo2_r,
        send_l,
        send_r,
        term_l,
        term_r,
        own_adj,
        norm_buf,
        obj_buf,
        tile_sem,
        in_sem,
        inv_sem,
        halo_send,
        halo_recv,
        norm_send,
        norm_recv,
        obj_send,
        obj_recv,
    ) = scratch[row_blocks:]
    rows = row_blocks * BLK
    ends = MB // 2
    own = primal_hbm.shape[0] // PAIR
    pairs = own + 2 * ends
    col_blocks = 2 * own
    total_blocks = col_blocks * n
    end_rows = ends * PAIR
    mid_rows = (own - 2 * ends) * PAIR

    me = lax.axis_index("band")
    left = lax.rem(me + n - 1, n)
    right = lax.rem(me + 1, n)

    barrier = pltpu.get_barrier_semaphore()

    def load_rows(start, size, k):
        return pltpu.make_async_copy(
            primal_hbm.at[pl.ds(start, size)], primal.at[pl.ds(start, size)], in_sem.at[k]
        )

    head = load_rows(0, end_rows, 0)
    tail = load_rows(end_rows + mid_rows, end_rows, 1)
    middle = load_rows(end_rows, mid_rows, 2)
    rhs_in = pltpu.make_async_copy(rhs_hbm, rhs, in_sem.at[3])
    dual_in = pltpu.make_async_copy(dual_hbm, dual, in_sem.at[4])
    tile_in = [
        pltpu.make_async_copy(
            tiles_hbm.at[g], tiles[g].at[pl.ds(0, tile_count)], tile_sem.at[g]
        )
        for g in range(row_blocks)
    ]
    head.start()
    tail.start()
    for k in [1, n - 1] + list(range(2, n - 1)):
        pl.semaphore_signal(
            barrier, inc=1, device_id={"band": lax.rem(me + k, n)}, device_id_type=MESH
        )
    rhs_in.start()
    for copy in tile_in[:2]:
        copy.start()
    middle.start()
    for copy in tile_in[2:]:
        copy.start()
    dual_in.start()

    def chunk(ref, c):
        return ref.at[pl.ds(c * PAIR, PAIR)]

    def exchange(kind, side, c, source, target):
        index = (kind * 2 + side) * ends + c
        return pltpu.make_async_remote_copy(
            src_ref=source,
            dst_ref=target,
            send_sem=halo_send.at[index],
            recv_sem=halo_recv.at[index],
            device_id={"band": left if side == 0 else right},
            device_id_type=MESH,
        )

    to_left = [exchange(0, 0, c, chunk(flow, c), chunk(halo_r, c)) for c in range(ends)]
    to_right = [
        exchange(0, 1, c, chunk(flow, own - ends + c), chunk(halo_l, c)) for c in range(ends)
    ]
    head.wait()
    for c in range(ends):
        flow[c * PAIR : (c + 1) * PAIR] = primal[c * PAIR : (c + 1) * PAIR].astype(BF16)
    tail.wait()
    for c in range(own - ends, own):
        flow[c * PAIR : (c + 1) * PAIR] = primal[c * PAIR : (c + 1) * PAIR].astype(BF16)
    pl.semaphore_wait(barrier, n - 1)
    for c in range(ends):
        to_left[c].start()
        to_right[c].start()

    def share(buf, send_sems, recv_sems, k, slot, peer):
        return pltpu.make_async_remote_copy(
            src_ref=buf.at[slot],
            dst_ref=buf.at[slot],
            send_sem=send_sems.at[k],
            recv_sem=recv_sems.at[k],
            device_id={"band": peer},
            device_id_type=MESH,
        )

    def share_all(buf, send_sems, recv_sems):
        copies = [
            share(buf, send_sems, recv_sems, k, me, lax.rem(me + k, n)) for k in range(1, n)
        ]
        for copy in copies:
            copy.start()
        return copies

    def collect_all(buf, send_sems, recv_sems):
        for k in range(1, n):
            source = lax.rem(me + n - k, n)
            share(buf, send_sems, recv_sems, k, source, lax.rem(me + k, n)).wait_recv()
        return jnp.sum(buf[...], axis=0)

    def stack(first, second):
        return jnp.concatenate([first, second, jnp.zeros((6, BLK), F32)], axis=0)

    rhs_in.wait()
    rhs_sq = jnp.sum(rhs[...] * rhs[...], axis=0, keepdims=True)
    cost_sq = jnp.sum(cost_ref[...] * cost_ref[...], axis=0, keepdims=True)
    norm_buf[me] = stack(rhs_sq, cost_sq)
    norm_copies = share_all(norm_buf, norm_send, norm_recv)

    base = me * col_blocks - MB
    local = lax.rem(ids_ref[...] - base + total_blocks, total_blocks)
    lane = lax.broadcasted_iota(jnp.int32, (row_blocks, BLK), 1)
    inverse = jnp.full((row_blocks, BLK), tile_count, jnp.int32)
    for t in range(tile_count):
        inverse = jnp.where(lane == local[:, t : t + 1], t, inverse)
    inv_v[...] = inverse
    inv_copy = pltpu.make_async_copy(inv_v, inv_s, inv_sem)
    inv_copy.start()

    for w in range(col_blocks):
        cost_col[w * BLK : (w + 1) * BLK] = jnp.transpose(
            jnp.broadcast_to(cost_ref[w : w + 1, :], (BLK, BLK))
        )
    middle.wait()
    for c in range(ends, own - ends):
        flow[c * PAIR : (c + 1) * PAIR] = primal[c * PAIR : (c + 1) * PAIR].astype(BF16)

    inv_copy.wait()
    for g in range(row_blocks):
        tiles[g][tile_count] = jnp.zeros((BLK, BLK), BF16)
        tile_in[g].wait()

        def place(p, carry, g=g):
            for half in range(2):
                start = pl.multiple_of((2 * p + half) * BLK, BLK)
                dense[g * BLK : (g + 1) * BLK, pl.ds(start, BLK)] = tiles[g][
                    inv_s[g, 2 * p + half]
                ]
            return carry

        lax.fori_loop(0, pairs, place, None, unroll=4)

    left_end = end_rows
    right_end = (ends + own) * PAIR
    part_rows = 2 * BLK

    def product(start, block, first=False):
        size = block.shape[0]

        def step(i, carry):
            at = pl.ds(pl.multiple_of(i * part_rows, part_rows), part_rows)
            value = jnp.dot(
                dense[at, start : start + size], block[...], preferred_element_type=F32
            )
            acc[at] = value if first else acc[at] + value
            return carry

        lax.fori_loop(0, rows // part_rows, step, None)

    def halo_products(low, low_copies, high, high_copies):
        half = ends // 2
        for h in range(2):
            for c in range(h * half, (h + 1) * half):
                low_copies[c].wait_recv()
                high_copies[c].wait_recv()
            at = h * half * PAIR
            for i in range(0, rows, part_rows):
                acc[i : i + part_rows] += jnp.dot(
                    dense[i : i + part_rows, at : at + half * PAIR],
                    low[at : at + half * PAIR],
                    preferred_element_type=F32,
                ) + jnp.dot(
                    dense[i : i + part_rows, right_end + at : right_end + at + half * PAIR],
                    high[at : at + half * PAIR],
                    preferred_element_type=F32,
                )

    product(left_end, flow, True)
    halo_products(halo_l, to_right, halo_r, to_left)

    norms = collect_all(norm_buf, norm_send, norm_recv)
    cost_total = jnp.sum(norms[1:2], axis=1, keepdims=True)
    omega = jnp.sqrt(cost_total / (norms[0:1] + 1e-06))
    tau = 0.3 / omega
    sigma = 0.3 * omega

    dual_in.wait()
    dual_mid = dual[...] + sigma * (rhs[...] - acc[...])
    dual[...] = dual_mid
    dual_t = jnp.transpose(dual_mid).astype(BF16)

    def adjoint(p):
        flat = jnp.dot(
            dual_t, dense[:, p * PAIR : (p + 1) * PAIR], preferred_element_type=F32
        )
        return jnp.transpose(flat)

    terms_left = [exchange(1, 0, c, chunk(send_l, c), chunk(term_r, c)) for c in range(ends)]
    terms_right = [exchange(1, 1, c, chunk(send_r, c), chunk(term_l, c)) for c in range(ends)]
    for c in range(ends):
        send_l[c * PAIR : (c + 1) * PAIR] = adjoint(c).astype(BF16)
        terms_left[c].start()
        send_r[c * PAIR : (c + 1) * PAIR] = adjoint(ends + own + c).astype(BF16)
        terms_right[c].start()

    for c in range(ends):
        own_adj[c] = adjoint(ends + c)
        own_adj[ends + c] = adjoint(own + c)

    def advance(p, total):
        span = slice(p * PAIR, (p + 1) * PAIR)
        start = primal[span]
        cost = cost_col[span]
        following = jnp.maximum(start - tau * (cost - total), 0.0)
        flow2[span] = (2.0 * following - start).astype(BF16)
        primal_out[span] = following
        return jnp.sum(cost * following, axis=0, keepdims=True)

    primal_obj = jnp.zeros((1, BLK), F32)
    for p in range(ends, own - ends):
        primal_obj += advance(p, adjoint(ends + p))
    product(left_end + end_rows, flow2.at[pl.ds(end_rows, mid_rows)], True)

    flow_left = [exchange(2, 0, c, chunk(flow2, c), chunk(halo2_r, c)) for c in range(ends)]
    flow_right = [
        exchange(2, 1, c, chunk(flow2, own - ends + c), chunk(halo2_l, c)) for c in range(ends)
    ]
    for c in range(ends):
        terms_right[c].wait_recv()
        primal_obj += advance(c, own_adj[c] + term_l[c * PAIR : (c + 1) * PAIR].astype(F32))
        flow_left[c].start()
        terms_left[c].wait_recv()
        primal_obj += advance(own - ends + c, own_adj[ends + c] + term_r[c * PAIR : (c + 1) * PAIR].astype(F32))
        flow_right[c].start()
    product(left_end, flow2.at[pl.ds(0, end_rows)])
    product(right_end - end_rows, flow2.at[pl.ds(end_rows + mid_rows, end_rows)])
    halo_products(halo2_l, flow_right, halo2_r, flow_left)

    dual_next = dual[...] + sigma * (rhs[...] - acc[...])
    dual_out[...] = dual_next
    dual_obj = jnp.sum(rhs[...] * dual_next, axis=0, keepdims=True)
    obj_buf[me] = stack(primal_obj, dual_obj)
    obj_copies = share_all(obj_buf, obj_send, obj_recv)
    for copy in norm_copies + to_left + to_right + terms_left + terms_right + flow_left + flow_right:
        copy.wait_send()
    totals_out[...] = collect_all(obj_buf, obj_send, obj_recv)
    for copy in obj_copies:
        copy.wait_send()


def finish(primal_in, dual_in, totals, primal_out, dual_out, gap_out, sems):
    parts = sems.shape[0] // 2
    copies = []
    for k in range(parts):
        for j, (source, target) in enumerate(((primal_in, primal_out), (dual_in, dual_out))):
            size = source.shape[0] // parts
            at = pl.ds(k * size, size)
            copies.append(
                pltpu.make_async_copy(source.at[at], target.at[at], sems.at[2 * k + j])
            )
    for copy in copies:
        copy.start()
    primal_total = totals[0:1]
    dual_total = totals[1:2]
    gap_out[...] = (primal_total - dual_total) / (
        1.0 + jnp.abs(primal_total) + jnp.abs(dual_total)
    )
    for copy in copies:
        copy.wait()


def per_device(n, tile_blocks, column_ids, arc_cost, demand_rhs, primal_start, dual_start):
    row_blocks, tile_count = column_ids.shape
    cols, scen = primal_start.shape
    rows = demand_rhs.shape[0]
    own = cols // PAIR
    ends = MB // 2
    pairs = own + 2 * ends
    any_space = pl.BlockSpec(memory_space=pl.ANY)
    hbm = pl.BlockSpec(memory_space=pltpu.HBM)
    vmem = pl.BlockSpec(memory_space=pltpu.VMEM)
    halo = pltpu.VMEM((ends * PAIR, scen), BF16)
    dma = pltpu.SemaphoreType.DMA
    scratch = [pltpu.VMEM((tile_count + 1, BLK, BLK), BF16) for _ in range(row_blocks)]
    scratch += [
        pltpu.VMEM((rows, pairs * PAIR), BF16),
        pltpu.VMEM((row_blocks, BLK), jnp.int32),
        pltpu.SMEM((row_blocks, BLK), jnp.int32),
        pltpu.VMEM((cols, scen), F32),
        pltpu.VMEM((cols, scen), F32),
        pltpu.VMEM((rows, scen), F32),
        pltpu.VMEM((rows, scen), F32),
        pltpu.VMEM((rows, scen), F32),
        pltpu.VMEM((cols, scen), BF16),
        pltpu.VMEM((cols, scen), BF16),
        halo,
        halo,
        halo,
        halo,
        halo,
        halo,
        halo,
        halo,
        pltpu.VMEM((2 * ends, PAIR, scen), F32),
        pltpu.VMEM((n, 8, scen), F32),
        pltpu.VMEM((n, 8, scen), F32),
        dma((row_blocks,)),
        dma((5,)),
        dma,
        dma((6 * ends,)),
        dma((6 * ends,)),
        dma((n,)),
        dma((n,)),
        dma((n,)),
        dma((n,)),
    ]
    flops = 3 * 2 * pairs * PAIR * rows * scen
    outs = pl.pallas_call(
        functools.partial(kernel, n),
        out_shape=(
            pltpu.VMEM((cols, scen), F32),
            pltpu.VMEM((rows, scen), F32),
            pltpu.VMEM((8, scen), F32),
        ),
        in_specs=[hbm, vmem, vmem, hbm, hbm, hbm],
        out_specs=(vmem, vmem, vmem),
        scratch_shapes=scratch,
        compiler_params=pltpu.CompilerParams(
            collective_id=0, has_side_effects=True, vmem_limit_bytes=56 * 1024 * 1024
        ),
        cost_estimate=pl.CostEstimate(
            flops=flops, bytes_accessed=2 * tile_blocks.size + 8 * cols * scen, transcendentals=0
        ),
    )(
        tile_blocks,
        column_ids,
        arc_cost.reshape(cols // BLK, BLK),
        demand_rhs,
        primal_start,
        dual_start,
    )
    primal_next, dual_next, gap = pl.pallas_call(
        finish,
        out_shape=(
            jax.ShapeDtypeStruct((cols, scen), F32),
            jax.ShapeDtypeStruct((rows, scen), F32),
            jax.ShapeDtypeStruct((1, scen), F32),
        ),
        in_specs=[any_space, any_space, vmem],
        out_specs=(hbm, hbm, vmem),
        scratch_shapes=[dma((8,))],
        compiler_params=pltpu.CompilerParams(vmem_limit_bytes=1024 * 1024),
    )(*outs)
    return primal_next, dual_next, gap.reshape(scen)


def solution(mesh):
    in_specs = (
        P(("groups", "band"), None, None, None),
        P(("groups", "band"), None),
        P(("groups", "band")),
        P(("groups", "band"), None),
        P(("groups", "band"), None),
        P(("groups", "band"), None),
    )
    out_specs = (P(("groups", "band"), None), P(("groups", "band"), None), P("groups"))
    return jax.shard_map(
        functools.partial(per_device, mesh.shape["band"]),
        mesh=mesh,
        in_specs=in_specs,
        out_specs=out_specs,
        check_vma=False,
    )
```
